32 devices in a mesh: dp: 8 (over z, x), head: 4 (over y, core).
Axes of the slice: x: 2, y: 2, z: 4, core: 2. Of those that a mesh axis runs over, the one named last changes fastest.
Arguments:
- tokens: bfloat16 [32, 512, 1024], P('dp', 'head'), may hold values from -6 to 6
- segments: int32 [32, 512], P('dp'), may hold values from -1 to 3, as said below
- cotangent: bfloat16 [32, 512, 1024], P('dp', 'head'), may hold values from -6 to 6
- qkv_weight: bfloat16 [1024, 3072], replicated, may hold values from -0.25 to 0.25
- query_bias: float32 [1024], replicated, may hold values from -3 to 3
- value_bias: float32 [1024], replicated, may hold values from -3 to 3
- out_weight: bfloat16 [1024, 1024], replicated, may hold values from -0.75 to 0.75
- out_bias: float32 [1024], replicated, may hold values from -3 to 3
- norm1_gain: float32 [1024], replicated, may hold values from 0.5 to 1.5
- norm1_bias: float32 [1024], replicated, may hold values from -3 to 3
- up_weight: bfloat16 [1024, 4096], replicated, may hold values from -0.1875 to 0.1875
- up_bias: float32 [4096], replicated, may hold values from -3 to 3
- down_weight: bfloat16 [4096, 1024], replicated, may hold values from -0.09375 to 0.09375
- down_bias: float32 [1024], replicated, may hold values from -3 to 3
- norm2_gain: float32 [1024], replicated, may hold values from 0.5 to 1.5
- norm2_bias: float32 [1024], replicated, may hold values from -3 to 3
Outputs:
- layer_out: bfloat16 [32, 512, 1024], P('dp', 'head')
- tokens_grad: bfloat16 [32, 512, 1024], P('dp', 'head')
- query_bias_grad: float32 [1024], replicated
- value_bias_grad: float32 [1024], replicated
- out_bias_grad: float32 [1024], replicated
- norm1_bias_grad: float32 [1024], replicated
- up_bias_grad: float32 [4096], replicated
- down_bias_grad: float32 [1024], replicated
- norm2_bias_grad: float32 [1024], replicated
The draws below stay inside these ranges and needn't reach their ends.
Inputs may be any that keep to these rules, and one draw needn't show every extreme that they name: `segments`: along each sequence the ids never fall until the padding, which fills the sequence's end with -1; of the 4 sequences of each index of dp, one holds a single document and no padding.
All inputs are finite; a program needn't handle non-finite values.
Results may differ from the reference program's by a relative error of at most 0.015.
Values may be sent and summed in bfloat16 or wider, within the bound.
A program may use at most 128 MiB of HBM per device.

```python
import math
import jax
import jax.numpy as jnp
from jax import lax

D = 1024
H = 16
HD = 64
FF = 4096
LEN = 512
SEQS_DEV = 4
SEQS = 32


def draw_segments(key, part):
    key = jax.random.fold_in(key, 11)
    key_pad, key_cut, key_pick = jax.random.split(key, 3)
    padding = jax.random.randint(key_pad, (SEQS, 1), 1, LEN // 8 + 1)
    live = LEN - padding
    raw_cuts = jax.random.randint(key_cut, (SEQS, 3), 0, 1 << 20)
    cuts = raw_cuts % (live - 1) + 1
    places = jnp.arange(LEN, dtype=jnp.int32)
    doc_ids = jnp.sum((places[None, :, None] >= cuts[:, None, :]).astype(jnp.int32), axis=-1)
    doc_ids = jnp.where(places[None, :] >= live, -1, doc_ids)
    picked = jax.random.randint(key_pick, (SEQS // SEQS_DEV, 1), 0, SEQS_DEV)
    whole_doc = (jnp.arange(SEQS_DEV, dtype=jnp.int32)[None, :] == picked).reshape(SEQS)
    return jnp.where(whole_doc[:, None], 0, doc_ids).astype(jnp.int32)


def levels(rng, extent, pieces, least, top_value):
    def one(position, shards_of):
        heights = jax.random.uniform(jax.random.fold_in(jax.random.fold_in(rng, 6), position), (shards_of,), jnp.float32, least / len(pieces), top_value / len(pieces))
        return jnp.repeat(jnp.exp(heights), extent[position] // shards_of).reshape((-1,) + (1,) * (len(extent) - position - 1))

    factor_of = one(*pieces[0])
    for cut in pieces[1:]:
        factor_of = factor_of * one(*cut)
    return factor_of


def normal_values(stream_key, extent, deviation, limit, cuts=(), kind=jnp.bfloat16):
    level = levels(stream_key, extent, cuts, -0.22, 0.18) if cuts else 1.0
    array = jax.random.normal(stream_key, extent, jnp.float32) * deviation * level
    return jnp.minimum(jnp.maximum(array, -limit), limit).astype(kind)


def setup_inputs(seed: int = 0) -> dict:
    seeds = jax.random.split(jax.random.key(seed), 17)
    return {
        "tokens": normal_values(seeds[0], (SEQS, LEN, D), 1.0, 6.0, ((0, 8), (1, 4))),
        "segments": draw_segments(jax.random.fold_in(seeds[16], 71), 0),
        "cotangent": normal_values(seeds[2], (SEQS, LEN, D), 1.0, 6.0, ((0, 8), (1, 4))),
        "qkv_weight": normal_values(seeds[3], (D, 3 * D), (D // 2) ** -0.5, 0.25),
        "query_bias": normal_values(seeds[4], (D,), 0.5, 3.0, (), jnp.float32),
        "value_bias": normal_values(seeds[5], (D,), 0.5, 3.0, (), jnp.float32),
        "out_weight": normal_values(seeds[6], (D, D), (D // 16) ** -0.5, 0.75),
        "out_bias": normal_values(seeds[7], (D,), 0.5, 3.0, (), jnp.float32),
        "norm1_gain": jnp.clip(1.0 + 0.1 * jax.random.normal(seeds[8], (D,), jnp.float32), 0.5, 1.5),
        "norm1_bias": normal_values(seeds[9], (D,), 0.5, 3.0, (), jnp.float32),
        "up_weight": normal_values(seeds[10], (D, FF), D ** -0.5, 0.1875),
        "up_bias": normal_values(seeds[11], (FF,), 0.5, 3.0, (), jnp.float32),
        "down_weight": normal_values(seeds[12], (FF, D), FF ** -0.5, 0.09375),
        "down_bias": normal_values(seeds[13], (D,), 0.5, 3.0, (), jnp.float32),
        "norm2_gain": jnp.clip(1.0 + 0.1 * jax.random.normal(seeds[14], (D,), jnp.float32), 0.5, 1.5),
        "norm2_bias": normal_values(seeds[15], (D,), 0.5, 3.0, (), jnp.float32),
    }


@jax.custom_vjp
def low(v):
    return lax.optimization_barrier(v.astype(jnp.bfloat16)).astype(jnp.float32)

@jax.custom_vjp
def low_back(v):
    return v

def low_keep(v):
    return (low(v), None)

def low_pass(kept, grad):
    return (grad,)

def back_keep(v):
    return (v, None)

def back_low(kept, grad):
    return (low(grad),)
low.defvjp(low_keep, low_pass)
low_back.defvjp(back_keep, back_low)
HIGH = lax.Precision.HIGHEST
NORM_EPS = 1e-05
NEG_FILL = -1e+30

def layer_norm(values, gain):
    centre = values - lax.optimization_barrier(jnp.mean(values, axis=-1, keepdims=True))
    spread = lax.optimization_barrier(jnp.mean(centre * centre, axis=-1, keepdims=True))
    return centre * lax.rsqrt(spread + NORM_EPS) * gain

def matmul(left, right):
    return jnp.dot(left, right, precision=HIGH)

def attend(item):
    stacked, doc_ids = item
    seq_len = stacked.shape[0]
    scale = 1.0 / math.sqrt(HD)
    queries = stacked[:, 0]
    key_part = stacked[:, 1]
    value_part = stacked[:, 2]
    scores = low_back(jnp.einsum('qhd,khd->hqk', queries, key_part, precision=HIGH) * scale)
    allowed = doc_ids[:, None] == doc_ids[None, :]
    scores = jnp.where(allowed[None], scores, NEG_FILL)
    row_max = lax.optimization_barrier(jnp.max(scores, axis=-1, keepdims=True))
    powers = jnp.exp(scores - row_max)
    chance = powers / lax.optimization_barrier(jnp.sum(powers, axis=-1, keepdims=True))
    context = jnp.einsum('hqk,khd->qhd', low(chance), value_part, precision=HIGH)
    return low(low_back(context)).reshape(seq_len, H * HD)

def forward(tok_group, query_bias, value_bias, out_bias, norm1_bias, up_bias, down_bias, norm2_bias, weights, doc_group):
    qkv_weight, out_weight, norm1_gain, up_weight, down_weight, norm2_gain = weights
    group_size, seq_len, model_width = tok_group.shape
    qkv_bias = jnp.concatenate([query_bias, jnp.zeros_like(query_bias), value_bias])
    projected = low(low_back(matmul(tok_group, qkv_weight) + qkv_bias))
    stacked = projected.reshape(group_size, seq_len, 3, H, HD)
    context = lax.map(jax.checkpoint(attend), (stacked, doc_group))
    attn_out = low_back(matmul(context, out_weight) + out_bias)
    hidden1 = layer_norm(tok_group + attn_out, norm1_gain) + norm1_bias
    inner = low_back(matmul(low(hidden1), up_weight) + up_bias)
    active = low(jax.nn.gelu(inner, approximate=False))
    branch = low_back(matmul(active, down_weight) + down_bias)
    return layer_norm(hidden1 + branch, norm2_gain) + norm2_bias

def reference(tokens, segments, cotangent, qkv_weight, query_bias, value_bias, out_weight, out_bias, norm1_gain, norm1_bias, up_weight, up_bias, down_weight, down_bias, norm2_gain, norm2_bias):
    weights = (qkv_weight.astype(jnp.float32), out_weight.astype(jnp.float32), norm1_gain.astype(jnp.float32), up_weight.astype(jnp.float32), down_weight.astype(jnp.float32), norm2_gain.astype(jnp.float32))
    biases = (query_bias.astype(jnp.float32), value_bias.astype(jnp.float32), out_bias.astype(jnp.float32), norm1_bias.astype(jnp.float32), up_bias.astype(jnp.float32), down_bias.astype(jnp.float32), norm2_bias.astype(jnp.float32))
    group_size = math.gcd(SEQS, 8)
    group_count = SEQS // group_size
    tok_all = tokens.astype(jnp.float32).reshape(group_count, group_size, LEN, D)
    cot_all = cotangent.astype(jnp.float32).reshape(group_count, group_size, LEN, D)
    doc_all = segments.reshape(group_count, group_size, LEN)

    def scan_step(totals, item):
        tok_group, doc_group, cot_group = item

        def run_layer(tok_value, *bias_values):
            return forward(tok_value, *bias_values, weights, doc_group)
        layer_value, pull_back = jax.vjp(run_layer, tok_group, *biases)
        gradients = pull_back(cot_group)
        totals = tuple((old + new for old, new in zip(totals, gradients[1:])))
        return (totals, (layer_value.astype(jnp.bfloat16), gradients[0].astype(jnp.bfloat16)))
    start = tuple((jnp.zeros(item.shape, jnp.float32) for item in biases))
    totals, (outs_all, grads_all) = lax.scan(scan_step, start, (tok_all, doc_all, cot_all))
    return (outs_all.reshape(SEQS, LEN, D), grads_all.reshape(SEQS, LEN, D), totals[0], totals[1], totals[2], totals[3], totals[4], totals[5], totals[6])
```

```python
import math

import jax
import jax.numpy as jnp
from jax import lax
from jax.sharding import PartitionSpec as P

HD = 64


NORM_EPS = 1e-05
NEG_FILL = -1e30


def layer_norm(values, gain):
    centre = values - jnp.mean(values, axis=-1, keepdims=True)
    spread = jnp.mean(centre * centre, axis=-1, keepdims=True)
    return centre * lax.rsqrt(spread + NORM_EPS) * gain


def times_transposed(left, right):
    return lax.dot_general(
        left, right, (((1,), (1,)), ((), ())), preferred_element_type=jnp.float32
    )


def masked_scores(stacked, doc_ids):
    seq_len = stacked.shape[0]
    heads_here = stacked.shape[2] // HD
    scale = 1.0 / math.sqrt(HD)
    queries = stacked[:, 0].reshape(seq_len, heads_here, HD)
    key_part = stacked[:, 1].reshape(seq_len, heads_here, HD)
    value_part = stacked[:, 2].reshape(seq_len, heads_here, HD)
    scores = (
        jnp.einsum("qhd,khd->hqk", queries, key_part, preferred_element_type=jnp.float32) * scale
    )
    allowed = doc_ids[:, None] == doc_ids[None, :]
    scores = jnp.where(allowed[None], scores, NEG_FILL)
    return (queries, key_part, value_part, scores)


def head_attend(item):
    stacked, doc_ids = item
    seq_len = stacked.shape[0]
    queries, key_part, value_part, scores = masked_scores(stacked, doc_ids)
    row_max = jnp.max(scores, axis=-1, keepdims=True)
    powers = jnp.exp(scores - row_max)
    row_sum = jnp.sum(powers, axis=-1, keepdims=True)
    chance = powers / row_sum
    context = jnp.einsum(
        "hqk,khd->qhd", chance.astype(jnp.bfloat16), value_part, preferred_element_type=jnp.float32
    )
    return (
        context.astype(jnp.bfloat16).reshape(seq_len, stacked.shape[2]),
        row_max + jnp.log(row_sum),
    )


def head_backward(item):
    stacked, doc_ids, log_total, ctx_grad = item
    seq_len = stacked.shape[0]
    width_here = stacked.shape[2]
    scale = 1.0 / math.sqrt(HD)
    queries, key_part, value_part, scores = masked_scores(stacked, doc_ids)
    chance = jnp.exp(scores - log_total)
    grad_heads = ctx_grad.reshape(seq_len, width_here // HD, HD)
    chance_grad = jnp.einsum(
        "qhd,khd->hqk", grad_heads, value_part, preferred_element_type=jnp.float32
    )
    row_dot = jnp.sum(chance * chance_grad, axis=-1, keepdims=True)
    score_grad = (chance * (chance_grad - row_dot)).astype(jnp.bfloat16)
    query_grad = (
        jnp.einsum("hqk,khd->qhd", score_grad, key_part, preferred_element_type=jnp.float32) * scale
    )
    key_grad = (
        jnp.einsum("hqk,qhd->khd", score_grad, queries, preferred_element_type=jnp.float32) * scale
    )
    value_grad = jnp.einsum(
        "hqk,qhd->khd", chance.astype(jnp.bfloat16), grad_heads, preferred_element_type=jnp.float32
    )
    joined = jnp.stack([query_grad, key_grad, value_grad], axis=1).astype(jnp.bfloat16)
    return joined.reshape(seq_len, 3, width_here)


def per_device(
    tokens,
    segments,
    cotangent,
    qkv_weight,
    query_bias,
    value_bias,
    out_weight,
    out_bias,
    norm1_gain,
    norm1_bias,
    up_weight,
    up_bias,
    down_weight,
    down_bias,
    norm2_gain,
    norm2_bias,
):
    seq_count, slice_len, model_width = tokens.shape
    seq_len = segments.shape[1]
    group = seq_len // slice_len
    mine = seq_count // group
    rows = mine * seq_len
    first = lax.axis_index("head") * mine
    doc_ids = lax.dynamic_slice_in_dim(segments, first, mine, axis=0)

    def to_sequences(values):
        return lax.all_to_all(values, "head", split_axis=0, concat_axis=1, tiled=True)

    def to_slices(values):
        return lax.all_to_all(values, "head", split_axis=1, concat_axis=0, tiled=True)

    flat_tokens = to_sequences(tokens).reshape(rows, model_width)
    out_grad_low = to_sequences(cotangent).reshape(rows, model_width)
    qkv_bias = jnp.concatenate([query_bias, jnp.zeros_like(query_bias), value_bias])
    projected = (
        jnp.dot(flat_tokens, qkv_weight, preferred_element_type=jnp.float32) + qkv_bias
    ).astype(jnp.bfloat16)
    head_stack = projected.reshape(mine, seq_len, 3, model_width)
    pairs = [head_attend((head_stack[i], doc_ids[i])) for i in range(mine)]
    ctx_tokens = jnp.concatenate([pair[0] for pair in pairs], axis=0)
    attn_out = jnp.dot(ctx_tokens, out_weight, preferred_element_type=jnp.float32) + out_bias
    resid_one = flat_tokens.astype(jnp.float32) + attn_out
    hidden1 = layer_norm(resid_one, norm1_gain) + norm1_bias
    hidden_low = hidden1.astype(jnp.bfloat16)
    inner = jnp.dot(hidden_low, up_weight, preferred_element_type=jnp.float32) + up_bias
    active = jax.nn.gelu(inner, approximate=False).astype(jnp.bfloat16)
    branch = jnp.dot(active, down_weight, preferred_element_type=jnp.float32) + down_bias
    resid_two = hidden1 + branch
    layer_out = (layer_norm(resid_two, norm2_gain) + norm2_bias).astype(jnp.bfloat16)
    layer_out = to_slices(layer_out.reshape(mine, seq_len, model_width))
    out_grad = out_grad_low.astype(jnp.float32)
    norm2_bias_grad = jnp.sum(out_grad, axis=0)
    norm_two_back = jax.vjp(lambda values: layer_norm(values, norm2_gain), resid_two)[1]
    resid2_grad = norm_two_back(out_grad)[0]
    branch_grad = resid2_grad.astype(jnp.bfloat16)
    down_bias_grad = jnp.sum(branch_grad.astype(jnp.float32), axis=0)
    active_grad = times_transposed(branch_grad, down_weight)
    gelu_back = jax.vjp(lambda values: jax.nn.gelu(values, approximate=False), inner)[1]
    inner_grad = gelu_back(active_grad)[0].astype(jnp.bfloat16)
    up_bias_grad = jnp.sum(inner_grad.astype(jnp.float32), axis=0)
    hidden1_grad = resid2_grad + times_transposed(inner_grad, up_weight)
    norm1_bias_grad = jnp.sum(hidden1_grad, axis=0)
    norm_one_back = jax.vjp(lambda values: layer_norm(values, norm1_gain), resid_one)[1]
    resid1_grad = norm_one_back(hidden1_grad)[0]
    attn_grad = resid1_grad.astype(jnp.bfloat16)
    out_bias_grad = jnp.sum(attn_grad.astype(jnp.float32), axis=0)
    ctx_grad = (
        times_transposed(attn_grad, out_weight)
        .astype(jnp.bfloat16)
        .reshape(mine, seq_len, model_width)
    )
    token_grad = jnp.concatenate(
        [head_backward((head_stack[i], doc_ids[i], pairs[i][1], ctx_grad[i])) for i in range(mine)],
        axis=0,
    ).reshape(rows, 3 * model_width)
    input_attn_grad = times_transposed(token_grad, qkv_weight)
    bias_sums = jnp.sum(token_grad.astype(jnp.float32), axis=0)
    query_bias_grad = bias_sums[:model_width]
    value_bias_grad = bias_sums[2 * model_width :]
    tokens_grad = to_slices(
        (resid1_grad + input_attn_grad).astype(jnp.bfloat16).reshape(mine, seq_len, model_width)
    )
    sums = lax.psum(
        (
            query_bias_grad,
            value_bias_grad,
            out_bias_grad,
            norm1_bias_grad,
            up_bias_grad,
            down_bias_grad,
            norm2_bias_grad,
        ),
        ("dp", "head"),
    )
    return (layer_out, tokens_grad) + tuple(sums)


def solution(mesh):
    in_specs = (
        P("dp", "head", None),
        P("dp", None),
        P("dp", "head", None),
        P(),
        P(),
        P(),
        P(),
        P(),
        P(),
        P(),
        P(),
        P(),
        P(),
        P(),
        P(),
        P(),
    )
    out_specs = (P("dp", "head", None), P("dp", "head", None), P(), P(), P(), P(), P(), P(), P())
    return jax.shard_map(
        per_device, mesh=mesh, in_specs=in_specs, out_specs=out_specs, check_vma=False
    )
```
